512 devices in a mesh: dp: 32 (over z_hi, x, core), tensor: 16 (over z_lo, y).
Axes of the slice: x: 4, y: 4, z: 16 (z_hi: 4, z_lo: 4; z = z_hi * 4 + z_lo), core: 2. Of those that a mesh axis runs over, the one named last changes fastest.
Arguments:
- gate_pre: bfloat16 [16384, 12800], P('dp', 'tensor'), may hold values from -8 to 8
- up_pre: bfloat16 [16384, 12800], P('dp', 'tensor'), may hold values from -6 to 6
- cotangent: bfloat16 [16384, 2560], P(('dp', 'tensor')), may hold values from -24 to 24
- down_weight: bfloat16 [12800, 2560], P('tensor', 'dp'), may hold values from -0.0546875 to 0.0546875
Outputs:
- grad_gate: bfloat16 [16384, 12800], P('dp', 'tensor')
- grad_up: bfloat16 [16384, 12800], P('dp', 'tensor')
- grad_down: bfloat16 [12800, 2560], P('tensor', 'dp')
- left_stat: float32 [16, 4, 800, 800], P('tensor', None, 'dp')
- right_stat: float32 [16, 4, 640, 640], P('tensor', None, 'dp')
The draws below stay inside these ranges and needn't reach their ends.
All inputs are finite; a program needn't handle non-finite values.
Results may differ from the reference program's by a relative error of at most 0.025.
Values may be sent and summed in bfloat16 or wider, within the bound.
A program may use at most 64 MiB of HBM per device.

```python
import math
import jax
import jax.numpy as jnp
from jax import lax

D = 2560
FF = 12800
BR = 800
CB = 640
TOK = 512
TOKENS = 16384
NR = 16
NC = 4
N_DP = 32


def spiked(array, key, source, target, shards_of, factor):
    owner, partner = [(jnp.arange(array.shape[dim]) // (array.shape[dim] // shards_of)).reshape([-1 if axis == dim else 1 for axis in range(array.ndim)]) for dim in (source, target)]
    chosen = jax.random.permutation(key, shards_of)[partner]
    strong = (owner == chosen) | (owner == (partner + shards_of // 2) % shards_of)
    return jnp.where(strong, factor * array, array)


def levels(stream_key, dims, cuts, least, high):
    gain = 1.0
    for position, blocks in cuts:
        heights = jax.random.uniform(jax.random.fold_in(jax.random.fold_in(stream_key, 6), position), (blocks,), jnp.float32, least / len(cuts), high / len(cuts))
        gain = gain * jnp.repeat(jnp.exp(heights), dims[position] // blocks).reshape((-1,) + (1,) * (len(dims) - 1 - position))
    return gain


def normal_values(stream_key, shape, width, most, pieces=(), kind=jnp.bfloat16):
    drawn = jax.random.normal(stream_key, shape, jnp.float32) * width
    if len(pieces) > 0:
        drawn = levels(stream_key, shape, pieces, -0.22, 0.18) * drawn
    return jnp.clip(drawn, min=-most, max=most).astype(kind)


def noise_with(key, extent, deviation, bound, shards, heavy, kind=jnp.bfloat16):
    values = deviation * jax.random.normal(key, extent, jnp.float32)
    if shards:
        values = values * levels(key, extent, shards, -0.22, 0.18)
    return jnp.clip(spiked(values, jax.random.fold_in(key, 3), *heavy), -bound, bound).astype(kind)


def setup_inputs(seed: int = 0) -> dict:
    key_of = jax.random.split(jax.random.key(seed), 5)
    return {
        "gate_pre": normal_values(key_of[0], (TOKENS, FF), 1.5, 8.0, ((0, 32), (1, 16))),
        "up_pre": normal_values(key_of[1], (TOKENS, FF), 1.0, 6.0, ((0, 32), (1, 16))),
        "cotangent": noise_with(key_of[2], (TOKENS, D), 1.0, 24.0, ((0, 512),), (0, 1, 512, 6.0)),
        "down_weight": normal_values(key_of[3], (FF, D), FF ** -0.5, 0.0546875, ((0, 16), (1, 32))),
    }


def reference(gate_pre, up_pre, cotangent, down_weight):
    scale = 1.0 / math.sqrt(TOKENS)
    weight_f = down_weight.astype(jnp.float32)
    gate_groups = gate_pre.reshape(N_DP, TOK, FF)
    up_groups = up_pre.reshape(N_DP, TOK, FF)
    cot_groups = cotangent.reshape(N_DP, TOK, D)

    def one_group(total, items):
        gate_g, up_g, cot_g = items
        gate_f = gate_g.astype(jnp.float32)
        up_f = up_g.astype(jnp.float32)
        sig = jax.nn.sigmoid(gate_f)
        act = gate_f * sig
        hidden = (act * up_f).astype(jnp.bfloat16)
        cot_f = cot_g.astype(jnp.float32)
        dh = jnp.dot(cot_f, weight_f.T, precision=lax.Precision.HIGHEST)
        grad_up = (dh * act).astype(jnp.bfloat16)
        grad_gate = (dh * up_f * sig * (1.0 + gate_f * (1.0 - sig))).astype(jnp.bfloat16)
        term = jnp.dot(hidden.astype(jnp.float32).T, cot_f, precision=lax.Precision.HIGHEST) * scale
        term = term.astype(jnp.bfloat16).astype(jnp.float32)
        return (total + term, (grad_gate, grad_up))
    start = jnp.zeros((FF, D), jnp.float32)
    summed, outs = lax.scan(one_group, start, (gate_groups, up_groups, cot_groups))
    grad_gate = outs[0].reshape(TOKENS, FF)
    grad_up = outs[1].reshape(TOKENS, FF)
    grad_down = summed.astype(jnp.bfloat16)
    blocks = grad_down.astype(jnp.float32).reshape(NR, BR, NC, CB)
    left_stat = jnp.einsum('rick,rjck->rcij', blocks, blocks, precision=lax.Precision.HIGHEST) / CB
    right_stat = jnp.einsum('rica,ricb->rcab', blocks, blocks, precision=lax.Precision.HIGHEST) / BR
    return (grad_gate, grad_up, grad_down, left_stat, right_stat)
```

```python
import jax
import jax.numpy as jnp
from jax import lax
from jax.experimental import pallas as pl
from jax.experimental.pallas import tpu as pltpu
from jax.sharding import PartitionSpec as P

D = 2560
BR = 800
CB = 640
TOK = 512
SCALE = 1.0 / 128.0
MESH = pl.DeviceIdType.MESH
F32 = jnp.float32
BF16 = jnp.bfloat16
NSEM = 120
ORDER = (2, 1, 3, 0)


def kernel(gate_h, up_h, cot_h, w_h, gg_h, gu_h, gd_ref, left_ref, right_ref,
           gate, up, wv, cot, ht, act, fac, wt, tb, cr, cs, xr, zs, z1r, z2r,
           gs, g2, sl, rl, sr, rr, acc, gg, gu, ssem, rsem, lsem):
    dp = lax.axis_index("dp")
    te = lax.axis_index("tensor")
    zh = dp // 8
    x = (dp // 2) % 4
    k = dp % 2
    zl = te // 4
    y = te % 4

    def at_zh(e):
        return (((zh + e) % 4) * 8 + x * 2 + k, te)

    def at_x(d):
        return (zh * 8 + ((x + d) % 4) * 2 + k, te)

    def at_core():
        return (zh * 8 + x * 2 + (1 - k), te)

    def at_zl(d):
        return (dp, (zl + d) * 4 + y)

    def at_y(d):
        return (dp, zl * 4 + (y + d) % 4)

    count = [0]
    sent = []

    def rcopy(src, dst, dev, sem=None):
        if sem is None:
            sem = count[0]
            count[0] += 1
        return pltpu.make_async_remote_copy(
            src_ref=src, dst_ref=dst, send_sem=ssem.at[sem], recv_sem=rsem.at[sem],
            device_id=dev, device_id_type=MESH)

    def send(src, dst, dev):
        c = rcopy(src, dst, dev)
        c.start()
        sent.append(c)
        return c

    loads_c = []
    for n, o in enumerate(ORDER):
        col = pl.multiple_of(((zh + o) % 4) * CB, CB)
        c = pltpu.make_async_copy(cot_h.at[:, pl.ds(col, CB)], cot.at[o, 0, y], lsem.at[n])
        c.start()
        loads_c.append(c)
    load_w = pltpu.make_async_copy(w_h, wv, lsem.at[4])
    load_w.start()
    loads_g = []
    for r in range(4):
        row = pl.multiple_of(((zl + r) % 4) * 128, 128)
        a = pltpu.make_async_copy(gate_h.at[pl.ds(row, 128)], gate.at[pl.ds(r * 128, 128)], lsem.at[5 + r])
        b = pltpu.make_async_copy(up_h.at[pl.ds(row, 128)], up.at[pl.ds(r * 128, 128)], lsem.at[9 + r])
        a.start()
        b.start()
        loads_g.append((a, b))

    bar = pltpu.get_barrier_semaphore()

    def greet(dev):
        pl.semaphore_signal(bar, inc=1, device_id=dev, device_id_type=MESH)

    greet(at_core())
    for d in (1, 2, 3):
        greet(at_y(d))
        greet(at_x(d))
        greet(at_zh(d))

    @pl.when(zl > 0)
    def _():
        greet(at_zl(-1))

    @pl.when(zl < 3)
    def _():
        greet(at_zl(1))

    load_w.wait()
    eye = (lax.broadcasted_iota(jnp.int32, (80, 80), 0) == lax.broadcasted_iota(jnp.int32, (80, 80), 1))
    wt[0, x, k] = lax.dot_general(
        eye.astype(F32).astype(BF16), wv[...], (((1,), (1,)), ((), ())),
        preferred_element_type=F32).astype(BF16)
    for c in loads_c:
        c.wait()

    pl.semaphore_wait(bar, 10 + jnp.where(zl > 0, 1, 0) + jnp.where(zl < 3, 1, 0))

    line_sem = {}
    for o in ORDER:
        for j in (1, 2, 3):
            for d in (1, -1):
                line_sem[o, j, d] = count[0]
                count[0] += 1

    def line_copy(o, j, d):
        if d == 1:
            s, t = (4 - (j - 1)) % 4, 4 - j
        else:
            s, t = j - 1, j
        return rcopy(cot.at[o, s, y], cot.at[o, t, y], at_zl(d), line_sem[o, j, d])

    def line_sends(o, j, d):
        if d == 1:
            return jnp.logical_and(zl - (j - 1) >= 0, zl < 3)
        return jnp.logical_and(zl + (j - 1) <= 3, zl > 0)

    def line_send(o, j):
        for d in (1, -1):
            @pl.when(line_sends(o, j, d))
            def _(d=d):
                line_copy(o, j, d).start()

    def line_recv(o, j):
        @pl.when(zl - j >= 0)
        def _():
            line_copy(o, j, 1).wait_recv()

        @pl.when(zl + j <= 3)
        def _():
            line_copy(o, j, -1).wait_recv()

    y_own = {}
    y_rest = {}
    for o in ORDER:
        line_send(o, 1)
        y_own[o] = [send(cot.at[o, 0, y], cot.at[o, 0, y], at_y(d)) for d in (1, 3, 2)]

    w_x = {}
    w_core = {}

    def w_to_x(o):
        w_x[o] = [send(wt.at[o, x, k], wt.at[o, x, k], at_x(d)) for d in (1, 3, 2)]

    def w_to_core(o):
        for c in w_x[o]:
            c.wait_recv()
        w_core[o] = send(wt.at[o, :, k], wt.at[o, :, k], at_core())

    w_to_x(0)

    def hidden(r):
        rows = pl.ds(r * 128, 128)
        loads_g[r][0].wait()
        loads_g[r][1].wait()
        g = gate[rows, :].astype(F32)
        u = up[rows, :].astype(F32)
        sig = jax.nn.sigmoid(g)
        a = g * sig
        act[rows, :] = a
        fac[rows, :] = u * sig * (1.0 + g * (1.0 - sig))
        ht[:, rows] = (a * u).astype(BF16).T

    def line_step(o, j):
        line_recv(o, j)
        if j < 3:
            line_send(o, j + 1)
        else:
            y_rest[o] = [send(cot.at[o, pl.ds(1, 3), y], cot.at[o, pl.ds(1, 3), y], at_y(d)) for d in (1, 3, 2)]

    hidden(0)
    line_step(2, 1)
    line_step(1, 1)
    hidden(1)
    line_step(2, 2)
    line_step(3, 1)
    line_step(1, 2)
    hidden(2)
    line_step(2, 3)
    line_step(0, 1)
    line_step(3, 2)
    line_step(1, 3)
    hidden(3)
    line_step(0, 2)
    line_step(3, 3)
    line_step(0, 3)

    w_up = send(wt.at[0, x, k], wt.at[3, x, k], at_zh(1))
    w_dn = send(wt.at[0, x, k], wt.at[1, x, k], at_zh(3))

    tb[:, pl.ds(4000, 96), :] = jnp.zeros((4, 96, 128), BF16)
    core_c = {}
    x_c = {}

    def stage1(o):
        for c in y_own[o]:
            c.wait_recv()
        for c in y_rest[o]:
            c.wait_recv()

        @pl.loop(0, 5)
        def _(i):
            m = pl.multiple_of(i * 160, 160)
            t = jnp.dot(ht[pl.ds(m, 160), :], cot[o].reshape(TOK, CB), preferred_element_type=F32) * SCALE
            for j in range(5):
                row = pl.multiple_of(j * 800 + i * 160, 160)
                tb[o, pl.ds(row, 160), :] = t[:, j * 128:(j + 1) * 128].astype(BF16)

        other = pl.multiple_of((1 - k) * 2048, 2048)
        core_c[o] = send(tb.at[o, pl.ds(other, 2048)], cr.at[o], at_core())

    def stage2(o):
        core_c[o].wait_recv()
        mine = pl.multiple_of(k * 2048, 2048)

        @pl.loop(0, 4)
        def _(i):
            m = pl.multiple_of(i * 512, 512)
            s = tb[o, pl.ds(mine + m, 512), :].astype(F32) + cr[o, pl.ds(m, 512), :].astype(F32)
            cs[o, i] = s.astype(BF16)

        x_c[o] = [send(cs.at[o, (x + d) % 4], xr.at[o, d - 1], at_x(d)) for d in (1, 3, 2)]

    def x_sum(o):
        for c in x_c[o]:
            c.wait_recv()
        return (cs[o, x].astype(F32) + xr[o, 0].astype(F32)) + (xr[o, 1].astype(F32) + xr[o, 2].astype(F32))

    z_c = {}

    def stage3(o):
        p = x_sum(o)
        if o == 2:
            zs[0] = p.astype(BF16)
            z_c["up"] = send(zs.at[0, pl.ds(0, 256)], z1r.at[0], at_zh(1))
            z_c["dn"] = send(zs.at[0, pl.ds(256, 256)], z1r.at[1], at_zh(3))
        elif o == 1:
            z_c["up"].wait_recv()
            zs[1, pl.ds(0, 256)] = (p[:256] + z1r[0].astype(F32)).astype(BF16)
            zs[1, pl.ds(256, 256)] = p[256:].astype(BF16)
            z_c["up2"] = send(zs.at[1], z2r.at[0], at_zh(1))
        elif o == 3:
            z_c["dn"].wait_recv()
            zs[2, pl.ds(0, 256)] = p[:256].astype(BF16)
            zs[2, pl.ds(256, 256)] = (p[256:] + z1r[1].astype(F32)).astype(BF16)
            z_c["dn2"] = send(zs.at[2], z2r.at[1], at_zh(3))
        else:
            z_c["up2"].wait_recv()
            z_c["dn2"].wait_recv()
            own = pl.multiple_of((k * 4 + x) * 512, 512)
            gs[pl.ds(own, 512), :] = (p + (z2r[0].astype(F32) + z2r[1].astype(F32))).astype(BF16)

    stage1(2)
    stage2(2)
    stage1(1)
    stage2(1)
    stage3(2)
    w_to_core(0)
    stage1(3)
    stage2(3)
    stage3(1)
    stage1(0)
    stage2(0)
    stage3(3)

    w_up.wait_recv()
    w_up2 = send(wt.at[3, x, k, pl.ds(0, 48)], wt.at[2, x, k, pl.ds(0, 48)], at_zh(1))
    w_dn.wait_recv()
    w_dn2 = send(wt.at[1, x, k, pl.ds(48, 32)], wt.at[2, x, k, pl.ds(48, 32)], at_zh(3))
    w_to_x(1)

    def dh_step(o, first):
        @pl.loop(0, 2)
        def _(i):
            c = cot[o, pl.ds(i * 2, 2)].reshape(256, CB)
            t = jnp.dot(c, wt[o].reshape(CB, BR), preferred_element_type=F32)
            rows = pl.ds(pl.multiple_of(i * 256, 256), 256)
            if first:
                acc[rows, :] = t
            else:
                acc[rows, :] += t

    w_core[0].wait_recv()
    dh_step(0, True)

    stage3(0)
    own = pl.multiple_of((k * 4 + x) * 512, 512)
    g_x = [send(gs.at[pl.ds(own, 512)], gs.at[pl.ds(own, 512)], at_x(d)) for d in (1, 3, 2)]
    w_to_x(3)
    w_to_core(1)
    for c in g_x:
        c.wait_recv()
    half = pl.multiple_of(k * 2048, 2048)
    g_core = send(gs.at[pl.ds(half, 2048)], gs.at[pl.ds(half, 2048)], at_core())
    w_up2.wait_recv()
    w_dn2.wait_recv()
    w_to_x(2)
    g_core.wait_recv()
    for j in range(5):
        g2[:, j * 128:(j + 1) * 128] = gs[pl.ds(j * 800, 800), :]

    def pick(n, per_zh, per_x, per_k, used):
        s = lax.broadcasted_iota(jnp.int32, (128, n), 0)
        r = lax.broadcasted_iota(jnp.int32, (128, n), 1)
        i = s & 31
        want = ((zh + (s >> 5)) & 3) * per_zh + x * per_x + k * per_k + i
        return jnp.logical_and(r == want, i < used).astype(F32).astype(BF16)

    gm = g2[...]
    rows_l = jnp.dot(pick(BR, 200, 50, 25, 25), gm, preferred_element_type=F32).astype(BF16)
    lt = lax.dot_general(rows_l, gm, (((1,), (1,)), ((), ())), preferred_element_type=F32) / CB
    cols_r = lax.dot_general(
        pick(CB, 160, 40, 20, 20), gm, (((1,), (1,)), ((), ())), preferred_element_type=F32).astype(BF16)
    rt = jnp.dot(cols_r, gm, preferred_element_type=F32) / BR
    for e in (1, 2, 3):
        sl[e - 1] = lt[32 * e:32 * e + 32].astype(BF16)
        sr[e - 1] = rt[32 * e:32 * e + 32].astype(BF16)
    st = {}
    for e in (2, 1, 3):
        st[e] = (send(sl.at[e - 1], rl.at[e - 1], at_zh(e)), send(sr.at[e - 1], rr.at[e - 1], at_zh(e)))
    left_ref[zh] = lt[:25]
    right_ref[zh] = rt[:20]
    sel = (lax.broadcasted_iota(jnp.int32, (CB, 80), 0)
           == lax.broadcasted_iota(jnp.int32, (CB, 80), 1) + (2 * x + k) * 80)
    gd_ref[...] = jnp.dot(gm, sel.astype(F32).astype(BF16), preferred_element_type=F32).astype(BF16)

    w_core[1].wait_recv()
    dh_step(1, False)
    w_to_core(3)
    w_core[3].wait_recv()
    dh_step(3, False)
    w_to_core(2)
    w_core[2].wait_recv()
    stores = []
    for i in range(2):
        c = cot[2, pl.ds(i * 2, 2)].reshape(256, CB)
        rows = pl.ds(i * 256, 256)
        dh = acc[rows, :] + jnp.dot(c, wt[2].reshape(CB, BR), preferred_element_type=F32)
        gu[rows, :] = (dh * act[rows, :]).astype(BF16)
        gg[rows, :] = (dh * fac[rows, :]).astype(BF16)
        for r in (2 * i, 2 * i + 1):
            row = pl.multiple_of(((zl + r) % 4) * 128, 128)
            a = pltpu.make_async_copy(gg.at[pl.ds(r * 128, 128)], gg_h.at[pl.ds(row, 128)], lsem.at[13 + r])
            b = pltpu.make_async_copy(gu.at[pl.ds(r * 128, 128)], gu_h.at[pl.ds(row, 128)], lsem.at[17 + r])
            a.start()
            b.start()
            stores += [a, b]

    for e in (1, 3, 2):
        st[e][0].wait_recv()
        st[e][1].wait_recv()
        c = (zh + 4 - e) % 4
        left_ref[c] = rl[e - 1, pl.ds(0, 32), :].astype(F32)[:25]
        right_ref[c] = rr[e - 1, pl.ds(0, 32), :].astype(F32)[:20]

    for c in stores:
        c.wait()
    for c in sent:
        c.wait_send()
    for o in ORDER:
        for j in (1, 2, 3):
            for d in (1, -1):
                @pl.when(line_sends(o, j, d))
                def _(o=o, j=j, d=d):
                    line_copy(o, j, d).wait_send()
    assert count[0] <= NSEM


def body(gate_pre, up_pre, cotangent, down_weight):
    anyspec = pl.BlockSpec(memory_space=pl.ANY)
    vspec = pl.BlockSpec(memory_space=pltpu.VMEM)
    v = pltpu.VMEM
    out = pl.pallas_call(
        kernel,
        out_shape=(
            jax.ShapeDtypeStruct((TOK, BR), BF16),
            jax.ShapeDtypeStruct((TOK, BR), BF16),
            jax.ShapeDtypeStruct((BR, 80), BF16),
            jax.ShapeDtypeStruct((4, 25, BR), F32),
            jax.ShapeDtypeStruct((4, 20, CB), F32),
        ),
        in_specs=[anyspec] * 4,
        out_specs=(anyspec, anyspec, vspec, vspec, vspec),
        scratch_shapes=[
            v((TOK, BR), BF16),
            v((TOK, BR), BF16),
            v((BR, 80), BF16),
            v((4, 4, 4, 32, CB), BF16),
            v((BR, TOK), BF16),
            v((TOK, BR), F32),
            v((TOK, BR), F32),
            v((4, 4, 2, 80, BR), BF16),
            v((4, 4096, 128), BF16),
            v((4, 2048, 128), BF16),
            v((4, 4, 512, 128), BF16),
            v((4, 3, 512, 128), BF16),
            v((3, 512, 128), BF16),
            v((2, 256, 128), BF16),
            v((2, 512, 128), BF16),
            v((4096, 128), BF16),
            v((BR, CB), BF16),
            v((3, 32, BR), BF16),
            v((3, 32, BR), BF16),
            v((3, 32, CB), BF16),
            v((3, 32, CB), BF16),
            v((TOK, BR), F32),
            v((TOK, BR), BF16),
            v((TOK, BR), BF16),
            pltpu.SemaphoreType.DMA((NSEM,)),
            pltpu.SemaphoreType.DMA((NSEM,)),
            pltpu.SemaphoreType.DMA((21,)),
        ],
        compiler_params=pltpu.CompilerParams(
            collective_id=0, has_side_effects=True, vmem_limit_bytes=56 * 2**20),
        cost_estimate=pl.CostEstimate(flops=4_600_000_000, bytes_accessed=6_000_000, transcendentals=410_000),
    )(gate_pre, up_pre, cotangent, down_weight)
    return out[0], out[1], out[2], out[3][None], out[4][None]


def solution(mesh):
    return jax.shard_map(
        body,
        mesh=mesh,
        in_specs=(
            P("dp", "tensor"),
            P("dp", "tensor"),
            P(("dp", "tensor"), None),
            P("tensor", "dp"),
        ),
        out_specs=(
            P("dp", "tensor"),
            P("dp", "tensor"),
            P("tensor", "dp"),
            P("tensor", None, "dp", None),
            P("tensor", None, "dp", None),
        ),
        check_vma=False,
    )
```

```python
import jax
import jax.numpy as jnp
from jax import lax
from jax.experimental import pallas as pl
from jax.experimental.pallas import tpu as pltpu
from jax.sharding import PartitionSpec as P

D = 2560
BR = 800
CB = 640
TOK = 512
SCALE = 1.0 / 128.0
MESH = pl.DeviceIdType.MESH
F32 = jnp.float32
BF16 = jnp.bfloat16
NSEM = 160
PARTS = ((0, 384, 3, 0, 304, 0, 0, 160), (384, 256, 2, 2432, 208, 1216, 304, 112))
SUBS = ((2, 0), (2, 1), (1, 0), (3, 0), (1, 1), (3, 1), (0, 0), (0, 1))
ORDER = (2, 1, 3, 0)


def kernel(gate_h, up_h, cot_h, w_h, gg_h, gu_h, gd_ref, left_ref, right_ref,
           gate, up, cot, ht, act, fac, wt, tb, cr, cs, xr, zs, z1r, z2r,
           gs, g2, sp, rp, lt4, rt4, acc, gg, gu, ssem, rsem, lsem):
    dp = lax.axis_index("dp")
    te = lax.axis_index("tensor")
    zh = dp // 8
    x = (dp // 2) % 4
    k = dp % 2
    zl = te // 4
    y = te % 4

    def at_zh(e):
        return (((zh + e) % 4) * 8 + x * 2 + k, te)

    def at_x(d):
        return (zh * 8 + ((x + d) % 4) * 2 + k, te)

    def at_core():
        return (zh * 8 + x * 2 + (1 - k), te)

    def at_zl(d):
        return (dp, (zl + d) * 4 + y)

    def at_y(d):
        return (dp, zl * 4 + (y + d) % 4)

    count = [0]
    sent = []

    def rcopy(src, dst, dev, sem=None):
        if sem is None:
            sem = count[0]
            count[0] += 1
        return pltpu.make_async_remote_copy(
            src_ref=src, dst_ref=dst, send_sem=ssem.at[sem], recv_sem=rsem.at[sem],
            device_id=dev, device_id_type=MESH)

    def send(src, dst, dev):
        c = rcopy(src, dst, dev)
        c.start()
        sent.append(c)
        return c

    loads_c = []
    for n, o in enumerate(ORDER):
        col = pl.multiple_of(((zh + o) % 4) * CB, CB)
        c = pltpu.make_async_copy(cot_h.at[:, pl.ds(col, CB)], cot.at[o, 0, y], lsem.at[n])
        c.start()
        loads_c.append(c)
    load_w = pltpu.make_async_copy(w_h, wt.at[0, x, k], lsem.at[4])
    load_w.start()
    loads_g = []
    for r in range(4):
        row = pl.multiple_of(((zl + r) % 4) * 128, 128)
        a = pltpu.make_async_copy(gate_h.at[:, pl.ds(row, 128)], gate.at[:, pl.ds(r * 128, 128)], lsem.at[5 + r])
        b = pltpu.make_async_copy(up_h.at[:, pl.ds(row, 128)], up.at[:, pl.ds(r * 128, 128)], lsem.at[9 + r])
        a.start()
        b.start()
        loads_g.append((a, b))

    bar = pltpu.get_barrier_semaphore()

    def greet(dev):
        pl.semaphore_signal(bar, inc=1, device_id=dev, device_id_type=MESH)

    greet(at_core())
    for d in (1, 2, 3):
        greet(at_y(d))
        greet(at_x(d))
        greet(at_zh(d))

    @pl.when(zl > 0)
    def _():
        greet(at_zl(-1))

    @pl.when(zl < 3)
    def _():
        greet(at_zl(1))

    load_w.wait()
    for c in loads_c:
        c.wait()

    pl.semaphore_wait(bar, 10 + jnp.where(zl > 0, 1, 0) + jnp.where(zl < 3, 1, 0))

    line_sem = {}
    for o in ORDER:
        for j in (1, 2, 3):
            for d in (1, -1):
                line_sem[o, j, d] = count[0]
                count[0] += 1

    def line_copy(o, j, d):
        if d == 1:
            s, t = (4 - (j - 1)) % 4, 4 - j
        else:
            s, t = j - 1, j
        return rcopy(cot.at[o, s, y], cot.at[o, t, y], at_zl(d), line_sem[o, j, d])

    def line_sends(o, j, d):
        if d == 1:
            return jnp.logical_and(zl - (j - 1) >= 0, zl < 3)
        return jnp.logical_and(zl + (j - 1) <= 3, zl > 0)

    def line_send(o, j):
        for d in (1, -1):
            @pl.when(line_sends(o, j, d))
            def _(d=d):
                line_copy(o, j, d).start()

    def line_recv(o, j):
        @pl.when(zl - j >= 0)
        def _():
            line_copy(o, j, 1).wait_recv()

        @pl.when(zl + j <= 3)
        def _():
            line_copy(o, j, -1).wait_recv()

    def y_pair(o, slots, y_from, half, cols):
        up = cot.at[o, slots, (y + y_from[0]) % 4, half[0], cols]
        dn = cot.at[o, slots, (y + y_from[1]) % 4, half[1], cols]
        return [send(up, up, at_y(1)), send(dn, dn, at_y(3))]

    whole = (pl.ds(0, 32), pl.ds(0, 32))
    halves = (pl.ds(0, 16), pl.ds(16, 16))
    y1 = {}
    y2 = {}

    def own_to_y():
        y1["own"] = y_pair(pl.ds(0, 4), pl.ds(0, 1), (0, 0), whole, pl.ds(0, CB))

    def own_relay():
        for c in y1["own"]:
            c.wait_recv()
        y2["own"] = y_pair(pl.ds(0, 4), pl.ds(0, 1), (3, 1), halves, pl.ds(0, CB))

    def rest_to_y(n):
        o, part = SUBS[n]
        y1[o, part] = y_pair(o, pl.ds(1, 3), (0, 0), whole, pl.ds(*PARTS[part][:2]))

    def rest_relay(n):
        o, part = SUBS[n]
        for c in y1[o, part]:
            c.wait_recv()
        y2[o, part] = y_pair(o, pl.ds(1, 3), (3, 1), halves, pl.ds(*PARTS[part][:2]))

    for o in ORDER[:3]:
        line_send(o, 1)
    own_to_y()

    w_x = {}
    w_core = {}

    def w_to_x(o):
        w_x[o] = [send(wt.at[o, x, k], wt.at[o, x, k], at_x(d)) for d in (1, 3, 2)]

    def w_to_core(o):
        for c in w_x[o]:
            c.wait_recv()
        w_core[o] = send(wt.at[o, :, k], wt.at[o, :, k], at_core())

    w_to_x(0)

    def hidden(r):
        cols = pl.ds(r * 128, 128)
        loads_g[r][0].wait()
        loads_g[r][1].wait()

        @pl.loop(0, 5)
        def _(i):
            rows = pl.ds(pl.multiple_of(i * 160, 160), 160)
            g = gate[rows, cols].astype(F32)
            u = up[rows, cols].astype(F32)
            sig = jax.nn.sigmoid(g)
            a = g * sig
            act[rows, cols] = a
            fac[rows, cols] = u * sig * (1.0 + g * (1.0 - sig))
            ht[rows, cols] = (a * u).astype(BF16)

    def line_step(o, j):
        line_recv(o, j)
        if j < 3:
            line_send(o, j + 1)

    hidden(0)
    line_step(2, 1)
    line_send(0, 1)
    line_step(1, 1)
    hidden(1)
    line_step(2, 2)
    line_step(3, 1)
    own_relay()
    hidden(2)
    line_step(0, 1)
    line_step(1, 2)
    line_step(2, 3)
    rest_to_y(0)
    rest_to_y(1)
    hidden(3)
    line_step(3, 2)
    line_step(0, 2)
    line_step(1, 3)
    rest_to_y(2)
    rest_relay(0)
    line_step(3, 3)
    rest_to_y(3)
    rest_relay(1)
    rest_to_y(4)
    line_step(0, 3)

    def w_z(name, src, dst, first, rows, e):
        w_zc[name] = send(wt.at[src, x, k, pl.ds(first, rows)], wt.at[dst, x, k, pl.ds(first, rows)], at_zh(e))

    w_zc = {}
    w_z("up", 0, 3, 0, 48, 1)
    w_z("dn", 0, 1, 48, 32, 3)
    w_z("up2", 0, 3, 48, 32, 1)
    w_z("dn2", 0, 1, 0, 48, 3)

    tb[:, pl.ds(2400, 32), :] = jnp.zeros((4, 32, 128), BF16)
    tb[:, pl.ds(4032, 64), :] = jnp.zeros((4, 64, 128), BF16)
    core_c = {}
    x_c = {}
    z_c = {}
    g_x = {}

    def at16(v):
        return pl.multiple_of(v, 16)

    def stage1(n):
        o, part = SUBS[n]
        c0, cols, tiles, base, rows, b2, b5, up_rows = PARTS[part]
        if n == 0:
            for c in y2["own"]:
                c.wait_recv()
        for c in y2[o, part]:
            c.wait_recv()

        @pl.loop(0, 2)
        def _(i):
            m = pl.multiple_of(i * 400, 16)
            c = cot[o, :, :, :, pl.ds(c0, cols)].reshape(TOK, cols)
            t = jnp.dot(ht[pl.ds(m, 400), :], c, preferred_element_type=F32) * SCALE
            for j in range(tiles):
                tb[o, pl.ds(at16(base + j * 800 + i * 400), 400), :] = t[:, j * 128:(j + 1) * 128].astype(BF16)

        core_c[n] = send(tb.at[o, pl.ds(at16(base + (1 - k) * (4 * rows)), 4 * rows)],
                         cr.at[o, pl.ds(b2, 4 * rows)], at_core())

    def stage2(n):
        o, part = SUBS[n]
        c0, cols, tiles, base, rows, b2, b5, up_rows = PARTS[part]
        core_c[n].wait_recv()

        @pl.loop(0, 4)
        def _(i):
            a = tb[o, pl.ds(at16(base + (k * 4 + i) * rows), rows), :]
            b = cr[o, pl.ds(at16(b2 + i * rows), rows), :]
            cs[o, pl.ds(at16(b2 + i * rows), rows), :] = (a.astype(F32) + b.astype(F32)).astype(BF16)

        x_c[n] = [send(cs.at[o, pl.ds(at16(b2 + ((x + d) % 4) * rows), rows)],
                       xr.at[o, d - 1, pl.ds(b5, rows)], at_x(d)) for d in (1, 3, 2)]

    def stage3(n):
        o, part = SUBS[n]
        c0, cols, tiles, base, rows, b2, b5, up_rows = PARTS[part]
        dn_rows = rows - up_rows
        for c in x_c[n]:
            c.wait_recv()
        here = pl.ds(b5, rows)
        up = pl.ds(b5, up_rows)
        dn = pl.ds(b5 + up_rows, dn_rows)
        p = cs[o, pl.ds(at16(b2 + x * rows), rows), :].astype(F32) + xr[o, 0, here].astype(F32)
        p = p + (xr[o, 1, here].astype(F32) + xr[o, 2, here].astype(F32))
        if o == 2:
            zs[0, here] = p.astype(BF16)
            z_c["up", part] = send(zs.at[0, up], z1r.at[0, up], at_zh(1))
            z_c["dn", part] = send(zs.at[0, dn], z1r.at[1, dn], at_zh(3))
        elif o == 1:
            z_c["up", part].wait_recv()
            zs[1, up] = (p[:up_rows] + z1r[0, up].astype(F32)).astype(BF16)
            zs[1, dn] = p[up_rows:].astype(BF16)
            z_c["up2", part] = send(zs.at[1, here], z2r.at[0, here], at_zh(1))
        elif o == 3:
            z_c["dn", part].wait_recv()
            zs[2, up] = p[:up_rows].astype(BF16)
            zs[2, dn] = (p[up_rows:] + z1r[1, dn].astype(F32)).astype(BF16)
            z_c["dn2", part] = send(zs.at[2, here], z2r.at[1, here], at_zh(3))
        else:
            z_c["up2", part].wait_recv()
            z_c["dn2", part].wait_recv()
            own = pl.ds(at16(base + (k * 4 + x) * rows), rows)
            gs[own, :] = (p + (z2r[0, here].astype(F32) + z2r[1, here].astype(F32))).astype(BF16)
            g_x[part] = [send(gs.at[own], gs.at[own], at_x(d)) for d in (1, 3, 2)]

    for n in range(8):
        if n + 2 < 8:
            rest_relay(n + 2)
        if n + 5 < 8:
            rest_to_y(n + 5)
        stage1(n)
        if n >= 1:
            stage2(n - 1)
        if n >= 3:
            stage3(n - 3)
        if n == 3:
            w_to_core(0)
        if n == 5:
            w_zc["up"].wait_recv()
            w_z("up3", 3, 2, 0, 48, 1)
            w_zc["dn"].wait_recv()
            w_z("dn3", 1, 2, 48, 32, 3)
    stage2(7)
    w_zc["dn2"].wait_recv()
    w_to_x(1)
    stage3(5)
    stage3(6)

    def dh_step(o, first):
        @pl.loop(0, 2)
        def _(i):
            c = cot[o, pl.ds(i * 2, 2)].reshape(256, CB)
            t = jnp.dot(c, wt[o].reshape(CB, BR), preferred_element_type=F32)
            rows = pl.ds(pl.multiple_of(i * 256, 256), 256)
            if first:
                acc[rows, :] = t
            else:
                acc[rows, :] += t

    w_core[0].wait_recv()
    dh_step(0, True)

    stage3(7)
    w_zc["up2"].wait_recv()
    w_to_x(3)
    w_zc["up3"].wait_recv()
    w_zc["dn3"].wait_recv()
    g_core = []
    for part in (0, 1):
        for c in g_x[part]:
            c.wait_recv()
        base, rows = PARTS[part][3:5]
        half = pl.ds(at16(base + k * (4 * rows)), 4 * rows)
        g_core.append(send(gs.at[half], gs.at[half], at_core()))
    w_to_core(1)
    w_to_x(2)
    for part in (0, 1):
        g_core[part].wait_recv()
        c0, cols, tiles, base = PARTS[part][:4]
        for j in range(tiles):
            g2[:, c0 + j * 128:c0 + (j + 1) * 128] = gs[pl.ds(base + j * 800, 800), :]

    def pick(n, per_zh, per_x, per_k, first, used):
        r = lax.broadcasted_iota(jnp.int32, (48, n), 1)
        i = lax.broadcasted_iota(jnp.int32, (48, n), 0) - first
        base = x * per_x + k * per_k
        parts = []
        for e in range(4):
            hit = jnp.logical_and(r == i + (base + ((zh + e) % 4) * per_zh), jnp.logical_and(i >= 0, i < used))
            parts.append(hit.astype(F32))
        return jnp.concatenate(parts, axis=0).astype(BF16)

    gm = g2[...]
    rows_l = jnp.dot(pick(BR, 200, 50, 25, 0, 25), gm, preferred_element_type=F32).astype(BF16)
    lt = lax.dot_general(rows_l, gm, (((1,), (1,)), ((), ())), preferred_element_type=F32) / CB
    cols_r = lax.dot_general(
        pick(CB, 160, 40, 20, 25, 20), gm, (((1,), (1,)), ((), ())), preferred_element_type=F32).astype(BF16)
    rt = jnp.dot(cols_r, gm, preferred_element_type=F32) / BR
    for e in (2, 1, 3):
        a = lt[48 * e:48 * e + 48]
        b = rt[48 * e:48 * e + 48]
        sp[e - 1, :, pl.ds(0, 640)] = (a[:, :640] + b).astype(BF16)
        tail = a[:, 768:800]
        none = jnp.zeros((25, 32), F32)
        first = jnp.concatenate([none, tail[:20], none[:3]], axis=0)
        second = jnp.concatenate([none, tail[20:25], none[:18]], axis=0)
        both = jnp.concatenate([first, second, jnp.zeros((48, 64), F32)], axis=1)
        sp[e - 1, :, pl.ds(640, 128)] = (a[:, 640:768] + both).astype(BF16)
    st = {}
    for e in (2, 1, 3):
        st[e] = send(sp.at[e - 1], rp.at[e - 1], at_zh(e))
    lt4[zh, pl.ds(0, 25), :] = lt[:25]
    rt4[zh, pl.ds(0, 20), :] = rt[25:45]
    sel = (lax.broadcasted_iota(jnp.int32, (80, CB), 1)
           == lax.broadcasted_iota(jnp.int32, (80, CB), 0) + (2 * x + k) * 80)
    gd_ref[...] = lax.dot_general(
        sel.astype(F32).astype(BF16), gm, (((1,), (1,)), ((), ())), preferred_element_type=F32).astype(BF16)

    w_core[1].wait_recv()
    dh_step(1, False)
    w_to_core(3)
    w_core[3].wait_recv()
    dh_step(3, False)
    w_to_core(2)
    w_core[2].wait_recv()
    stores = []
    for i in range(2):
        c = cot[2, pl.ds(i * 2, 2)].reshape(256, CB)
        rows = pl.ds(i * 256, 256)
        dh = (acc[rows, :] + jnp.dot(c, wt[2].reshape(CB, BR), preferred_element_type=F32)).T
        gu[:, rows] = (dh * act[:, rows]).astype(BF16)
        gg[:, rows] = (dh * fac[:, rows]).astype(BF16)
        for r in (2 * i, 2 * i + 1):
            col = pl.multiple_of(((zl + r) % 4) * 128, 128)
            a = pltpu.make_async_copy(gg.at[:, pl.ds(r * 128, 128)], gg_h.at[:, pl.ds(col, 128)], lsem.at[13 + r])
            b = pltpu.make_async_copy(gu.at[:, pl.ds(r * 128, 128)], gu_h.at[:, pl.ds(col, 128)], lsem.at[17 + r])
            a.start()
            b.start()
            stores += [a, b]

    for e in (1, 3, 2):
        st[e].wait_recv()
        c = (zh + 4 - e) % 4
        v = rp[e - 1].astype(F32)
        lt4[c, pl.ds(0, 25), pl.ds(0, 768)] = v[:25]
        lt4[c, pl.ds(0, 20), pl.ds(768, 32)] = v[25:45, 640:672]
        lt4[c, pl.ds(20, 5), pl.ds(768, 32)] = v[25:30, 672:704]
        rt4[c, pl.ds(0, 20), :] = v[25:45, :640]
    for c in range(4):
        left_ref[:, c, :] = lt4[c, pl.ds(0, 25), :]
        right_ref[:, c, :] = rt4[c, pl.ds(0, 20), :]

    for c in stores:
        c.wait()
    for c in sent:
        c.wait_send()
    for o in ORDER:
        for j in (1, 2, 3):
            for d in (1, -1):
                @pl.when(line_sends(o, j, d))
                def _(o=o, j=j, d=d):
                    line_copy(o, j, d).wait_send()
    assert count[0] <= NSEM


def place(*refs):
    n = len(refs) // 3
    held, sem = refs[2 * n:3 * n], refs[3 * n]
    into = [pltpu.make_async_copy(refs[i], held[i], sem.at[i]) for i in range(n)]
    out = [pltpu.make_async_copy(held[i], refs[n + i], sem.at[n + i]) for i in range(n)]
    for c in into:
        c.start()
    for c, d in zip(into, out):
        c.wait()
        d.start()
    for d in out:
        d.wait()


def body(gate_pre, up_pre, cotangent, down_weight):
    anyspec = pl.BlockSpec(memory_space=pl.ANY)
    vspec = pl.BlockSpec(memory_space=pltpu.VMEM)
    v = pltpu.VMEM
    out = pl.pallas_call(
        kernel,
        out_shape=(
            jax.ShapeDtypeStruct((BR, TOK), BF16),
            jax.ShapeDtypeStruct((BR, TOK), BF16),
            jax.ShapeDtypeStruct((80, BR), BF16),
            jax.ShapeDtypeStruct((25, 4, BR), F32),
            jax.ShapeDtypeStruct((20, 4, CB), F32),
        ),
        in_specs=[anyspec] * 4,
        out_specs=(anyspec, anyspec, vspec, vspec, vspec),
        scratch_shapes=[
            v((BR, TOK), BF16),
            v((BR, TOK), BF16),
            v((4, 4, 4, 32, CB), BF16),
            v((BR, TOK), BF16),
            v((BR, TOK), F32),
            v((BR, TOK), F32),
            v((4, 4, 2, 80, BR), BF16),
            v((4, 4096, 128), BF16),
            v((4, 2048, 128), BF16),
            v((4, 2048, 128), BF16),
            v((4, 3, 512, 128), BF16),
            v((3, 512, 128), BF16),
            v((2, 512, 128), BF16),
            v((2, 512, 128), BF16),
            v((4096, 128), BF16),
            v((BR, CB), BF16),
            v((3, 48, 768), BF16),
            v((3, 48, 768), BF16),
            v((4, 32, BR), F32),
            v((4, 32, CB), F32),
            v((TOK, BR), F32),
            v((BR, TOK), BF16),
            v((BR, TOK), BF16),
            pltpu.SemaphoreType.DMA((NSEM,)),
            pltpu.SemaphoreType.DMA((NSEM,)),
            pltpu.SemaphoreType.DMA((21,)),
        ],
        compiler_params=pltpu.CompilerParams(
            collective_id=0, has_side_effects=True, vmem_limit_bytes=56 * 2**20),
        cost_estimate=pl.CostEstimate(flops=4_600_000_000, bytes_accessed=6_000_000, transcendentals=410_000),
    )(gate_pre.T, up_pre.T, cotangent, down_weight.T)
    out = pl.pallas_call(
        place,
        out_shape=tuple(jax.ShapeDtypeStruct(o.shape, o.dtype) for o in out),
        in_specs=[anyspec] * 5,
        out_specs=(anyspec,) * 5,
        scratch_shapes=[v(o.shape, o.dtype) for o in out] + [pltpu.SemaphoreType.DMA((10,))],
        compiler_params=pltpu.CompilerParams(vmem_limit_bytes=56 * 2**20),
    )(*out)
    return (out[0].T, out[1].T, out[2].T,
            out[3].transpose(1, 0, 2)[None], out[4].transpose(1, 0, 2)[None])


def solution(mesh):
    return jax.shard_map(
        body,
        mesh=mesh,
        in_specs=(
            P("dp", "tensor"),
            P("dp", "tensor"),
            P(("dp", "tensor"), None),
            P("tensor", "dp"),
        ),
        out_specs=(
            P("dp", "tensor"),
            P("dp", "tensor"),
            P("tensor", "dp"),
            P("tensor", None, "dp", None),
            P("tensor", None, "dp", None),
        ),
        check_vma=False,
    )
```

```python
import jax
import jax.numpy as jnp
from jax import lax
from jax.experimental import pallas as pl
from jax.experimental.pallas import tpu as pltpu
from jax.sharding import PartitionSpec as P

D = 2560
BR = 800
CB = 640
TOK = 512
SCALE = 1.0 / 128.0
MESH = pl.DeviceIdType.MESH
F32 = jnp.float32
BF16 = jnp.bfloat16
NSEM = 160
PARTS = ((0, 384, 3, 0, 304, 0, 0, 160), (384, 256, 2, 2432, 208, 1216, 304, 112))
SUBS = ((2, 0), (2, 1), (1, 0), (3, 0), (1, 1), (3, 1), (0, 0), (0, 1))
ORDER = (2, 1, 3, 0)


def kernel(gate_h, up_h, cot_h, w_h, gg_h, gu_h, gd_ref, left_ref, right_ref,
           gate, up, cot, ht, act, fac, wt, tb, cr, cs, xr, zs, z1r, z2r,
           gs, g2, sp, rp, lt4, rt4, acc, gg, gu, ssem, rsem, lsem):
    dp = lax.axis_index("dp")
    te = lax.axis_index("tensor")
    zh = dp // 8
    x = (dp // 2) % 4
    k = dp % 2
    zl = te // 4
    y = te % 4

    def at_zh(e):
        return (((zh + e) % 4) * 8 + x * 2 + k, te)

    def at_x(d):
        return (zh * 8 + ((x + d) % 4) * 2 + k, te)

    def at_core():
        return (zh * 8 + x * 2 + (1 - k), te)

    def at_zl(d):
        return (dp, (zl + d) * 4 + y)

    def at_y(d):
        return (dp, zl * 4 + (y + d) % 4)

    count = [0]
    sent = []

    def rcopy(src, dst, dev, sem=None):
        if sem is None:
            sem = count[0]
            count[0] += 1
        return pltpu.make_async_remote_copy(
            src_ref=src, dst_ref=dst, send_sem=ssem.at[sem], recv_sem=rsem.at[sem],
            device_id=dev, device_id_type=MESH)

    def send(src, dst, dev):
        c = rcopy(src, dst, dev)
        c.start()
        sent.append(c)
        return c

    loads_c = []
    for n, o in enumerate(ORDER):
        col = pl.multiple_of(((zh + o) % 4) * CB, CB)
        c = pltpu.make_async_copy(cot_h.at[:, pl.ds(col, CB)], cot.at[o, 0, y], lsem.at[n])
        c.start()
        loads_c.append(c)
    load_w = pltpu.make_async_copy(w_h, wt.at[0, x, k], lsem.at[4])
    load_w.start()
    loads_g = []
    for r in range(4):
        row = pl.multiple_of(((zl + r) % 4) * 128, 128)
        a = pltpu.make_async_copy(gate_h.at[:, pl.ds(row, 128)], gate.at[:, pl.ds(r * 128, 128)], lsem.at[5 + r])
        b = pltpu.make_async_copy(up_h.at[:, pl.ds(row, 128)], up.at[:, pl.ds(r * 128, 128)], lsem.at[9 + r])
        a.start()
        b.start()
        loads_g.append((a, b))

    bar = pltpu.get_barrier_semaphore()

    def greet(dev):
        pl.semaphore_signal(bar, inc=1, device_id=dev, device_id_type=MESH)

    greet(at_core())
    for d in (1, 2, 3):
        greet(at_y(d))
        greet(at_x(d))
        greet(at_zh(d))

    @pl.when(zl > 0)
    def _():
        greet(at_zl(-1))

    @pl.when(zl < 3)
    def _():
        greet(at_zl(1))

    load_w.wait()
    for c in loads_c:
        c.wait()

    pl.semaphore_wait(bar, 10 + jnp.where(zl > 0, 1, 0) + jnp.where(zl < 3, 1, 0))

    line_sem = {}
    for o in ORDER:
        for j in (1, 2, 3):
            for d in (1, -1):
                line_sem[o, j, d] = count[0]
                count[0] += 1

    def line_copy(o, j, d):
        if d == 1:
            s, t = (4 - (j - 1)) % 4, 4 - j
        else:
            s, t = j - 1, j
        return rcopy(cot.at[o, s, y], cot.at[o, t, y], at_zl(d), line_sem[o, j, d])

    def line_sends(o, j, d):
        if d == 1:
            return jnp.logical_and(zl - (j - 1) >= 0, zl < 3)
        return jnp.logical_and(zl + (j - 1) <= 3, zl > 0)

    def line_send(o, j):
        for d in (1, -1):
            @pl.when(line_sends(o, j, d))
            def _(d=d):
                line_copy(o, j, d).start()

    def line_recv(o, j):
        @pl.when(zl - j >= 0)
        def _():
            line_copy(o, j, 1).wait_recv()

        @pl.when(zl + j <= 3)
        def _():
            line_copy(o, j, -1).wait_recv()

    def y_pair(o, slots, y_from, half, cols):
        up = cot.at[o, slots, (y + y_from[0]) % 4, half[0], cols]
        dn = cot.at[o, slots, (y + y_from[1]) % 4, half[1], cols]
        return [send(up, up, at_y(1)), send(dn, dn, at_y(3))]

    whole = (pl.ds(0, 32), pl.ds(0, 32))
    halves = (pl.ds(0, 16), pl.ds(16, 16))
    y1 = {}
    y2 = {}

    def own_to_y():
        y1["own"] = y_pair(pl.ds(0, 4), pl.ds(0, 1), (0, 0), whole, pl.ds(0, CB))

    def own_relay():
        for c in y1["own"]:
            c.wait_recv()
        y2["own"] = y_pair(pl.ds(0, 4), pl.ds(0, 1), (3, 1), halves, pl.ds(0, CB))

    def rest_to_y(n):
        o, part = SUBS[n]
        y1[o, part] = y_pair(o, pl.ds(1, 3), (0, 0), whole, pl.ds(*PARTS[part][:2]))

    def rest_relay(n):
        o, part = SUBS[n]
        for c in y1[o, part]:
            c.wait_recv()
        y2[o, part] = y_pair(o, pl.ds(1, 3), (3, 1), halves, pl.ds(*PARTS[part][:2]))

    for o in ORDER[:3]:
        line_send(o, 1)
    own_to_y()

    w_x = {}
    w_core = {}

    def w_to_x(o):
        w_x[o] = [send(wt.at[o, x, k], wt.at[o, x, k], at_x(d)) for d in (1, 3, 2)]

    def w_to_core(o):
        for c in w_x[o]:
            c.wait_recv()
        w_core[o] = send(wt.at[o, :, k], wt.at[o, :, k], at_core())

    w_to_x(0)

    def hidden(r):
        cols = pl.ds(r * 128, 128)
        loads_g[r][0].wait()
        loads_g[r][1].wait()

        @pl.loop(0, 5)
        def _(i):
            rows = pl.ds(pl.multiple_of(i * 160, 160), 160)
            g = gate[rows, cols].astype(F32)
            u = up[rows, cols].astype(F32)
            sig = jax.nn.sigmoid(g)
            a = g * sig
            act[rows, cols] = a
            fac[rows, cols] = u * sig * (1.0 + g * (1.0 - sig))
            ht[rows, cols] = (a * u).astype(BF16)

    def line_step(o, j):
        line_recv(o, j)
        if j < 3:
            line_send(o, j + 1)

    hidden(0)
    line_step(2, 1)
    line_send(0, 1)
    line_step(1, 1)
    hidden(1)
    line_step(2, 2)
    line_step(3, 1)
    own_relay()
    hidden(2)
    line_step(0, 1)
    line_step(1, 2)
    line_step(2, 3)
    rest_to_y(0)
    rest_to_y(1)
    hidden(3)
    line_step(3, 2)
    line_step(0, 2)
    line_step(1, 3)
    rest_to_y(2)
    rest_relay(0)
    line_step(3, 3)
    rest_to_y(3)
    rest_relay(1)
    rest_to_y(4)
    line_step(0, 3)

    def w_z(name, src, dst, first, rows, e):
        w_zc[name] = send(wt.at[src, x, k, pl.ds(first, rows)], wt.at[dst, x, k, pl.ds(first, rows)], at_zh(e))

    w_zc = {}
    w_z("up", 0, 3, 0, 48, 1)
    w_z("dn", 0, 1, 48, 32, 3)
    w_z("up2", 0, 3, 48, 32, 1)
    w_z("dn2", 0, 1, 0, 48, 3)

    tb[:, pl.ds(2400, 32), :] = jnp.zeros((4, 32, 128), BF16)
    tb[:, pl.ds(4032, 64), :] = jnp.zeros((4, 64, 128), BF16)
    core_c = {}
    x_c = {}
    z_c = {}
    g_x = {}

    def at16(v):
        return pl.multiple_of(v, 16)

    def stage1(n):
        o, part = SUBS[n]
        c0, cols, tiles, base, rows, b2, b5, up_rows = PARTS[part]
        if n == 0:
            for c in y2["own"]:
                c.wait_recv()
        for c in y2[o, part]:
            c.wait_recv()

        @pl.loop(0, 2)
        def _(i):
            m = pl.multiple_of(i * 400, 16)
            c = cot[o, :, :, :, pl.ds(c0, cols)].reshape(TOK, cols)
            t = jnp.dot(ht[pl.ds(m, 400), :], c, preferred_element_type=F32) * SCALE
            for j in range(tiles):
                tb[o, pl.ds(at16(base + j * 800 + i * 400), 400), :] = t[:, j * 128:(j + 1) * 128].astype(BF16)

        core_c[n] = send(tb.at[o, pl.ds(at16(base + (1 - k) * (4 * rows)), 4 * rows)],
                         cr.at[o, pl.ds(b2, 4 * rows)], at_core())

    def stage2(n):
        o, part = SUBS[n]
        c0, cols, tiles, base, rows, b2, b5, up_rows = PARTS[part]
        core_c[n].wait_recv()

        @pl.loop(0, 4)
        def _(i):
            a = tb[o, pl.ds(at16(base + (k * 4 + i) * rows), rows), :]
            b = cr[o, pl.ds(at16(b2 + i * rows), rows), :]
            cs[o, pl.ds(at16(b2 + i * rows), rows), :] = (a.astype(F32) + b.astype(F32)).astype(BF16)

        x_c[n] = [send(cs.at[o, pl.ds(at16(b2 + ((x + d) % 4) * rows), rows)],
                       xr.at[o, d - 1, pl.ds(b5, rows)], at_x(d)) for d in (1, 3, 2)]

    def stage3(n):
        o, part = SUBS[n]
        c0, cols, tiles, base, rows, b2, b5, up_rows = PARTS[part]
        dn_rows = rows - up_rows
        for c in x_c[n]:
            c.wait_recv()
        here = pl.ds(b5, rows)
        up = pl.ds(b5, up_rows)
        dn = pl.ds(b5 + up_rows, dn_rows)
        p = cs[o, pl.ds(at16(b2 + x * rows), rows), :].astype(F32) + xr[o, 0, here].astype(F32)
        p = p + (xr[o, 1, here].astype(F32) + xr[o, 2, here].astype(F32))
        if o == 2:
            zs[0, here] = p.astype(BF16)
            z_c["up", part] = send(zs.at[0, up], z1r.at[0, up], at_zh(1))
            z_c["dn", part] = send(zs.at[0, dn], z1r.at[1, dn], at_zh(3))
        elif o == 1:
            z_c["up", part].wait_recv()
            zs[1, up] = (p[:up_rows] + z1r[0, up].astype(F32)).astype(BF16)
            zs[1, dn] = p[up_rows:].astype(BF16)
            z_c["up2", part] = send(zs.at[1, here], z2r.at[0, here], at_zh(1))
        elif o == 3:
            z_c["dn", part].wait_recv()
            zs[2, up] = p[:up_rows].astype(BF16)
            zs[2, dn] = (p[up_rows:] + z1r[1, dn].astype(F32)).astype(BF16)
            z_c["dn2", part] = send(zs.at[2, here], z2r.at[1, here], at_zh(3))
        else:
            z_c["up2", part].wait_recv()
            z_c["dn2", part].wait_recv()
            own = pl.ds(at16(base + (k * 4 + x) * rows), rows)
            gs[own, :] = (p + (z2r[0, here].astype(F32) + z2r[1, here].astype(F32))).astype(BF16)
            g_x[part] = [send(gs.at[own], gs.at[own], at_x(d)) for d in (1, 3, 2)]

    for n in range(8):
        if n + 2 < 8:
            rest_relay(n + 2)
        if n + 5 < 8:
            rest_to_y(n + 5)
        stage1(n)
        if n >= 1:
            stage2(n - 1)
        if n >= 3:
            stage3(n - 3)
        if n == 3:
            w_to_core(0)
        if n == 5:
            w_zc["up"].wait_recv()
            w_z("up3", 3, 2, 0, 48, 1)
            w_zc["dn"].wait_recv()
            w_z("dn3", 1, 2, 48, 32, 3)
        if n == 6:
            w_zc["dn2"].wait_recv()
            w_to_x(1)
    stage2(7)
    w_zc["up2"].wait_recv()
    w_to_x(3)
    stage3(5)
    stage3(6)

    def dh_step(o, first):
        @pl.loop(0, 2)
        def _(i):
            c = cot[o, pl.ds(i * 2, 2)].reshape(256, CB)
            t = jnp.dot(c, wt[o].reshape(CB, BR), preferred_element_type=F32)
            rows = pl.ds(pl.multiple_of(i * 256, 256), 256)
            if first:
                acc[rows, :] = t
            else:
                acc[rows, :] += t

    w_core[0].wait_recv()
    dh_step(0, True)

    stage3(7)
    w_zc["up3"].wait_recv()
    w_zc["dn3"].wait_recv()
    w_to_x(2)
    w_to_core(1)
    g_core = []
    for part in (0, 1):
        for c in g_x[part]:
            c.wait_recv()
        base, rows = PARTS[part][3:5]
        half = pl.ds(at16(base + k * (4 * rows)), 4 * rows)
        g_core.append(send(gs.at[half], gs.at[half], at_core()))
    w_to_core(3)
    for part in (0, 1):
        g_core[part].wait_recv()
        c0, cols, tiles, base = PARTS[part][:4]
        for j in range(tiles):
            g2[:, c0 + j * 128:c0 + (j + 1) * 128] = gs[pl.ds(base + j * 800, 800), :]

    def pick(n, per_zh, per_x, per_k, first, used):
        r = lax.broadcasted_iota(jnp.int32, (48, n), 1)
        i = lax.broadcasted_iota(jnp.int32, (48, n), 0) - first
        base = x * per_x + k * per_k
        parts = []
        for e in range(4):
            hit = jnp.logical_and(r == i + (base + ((zh + e) % 4) * per_zh), jnp.logical_and(i >= 0, i < used))
            parts.append(hit.astype(F32))
        return jnp.concatenate(parts, axis=0).astype(BF16)

    gm = g2[...]
    rows_l = jnp.dot(pick(BR, 200, 50, 25, 0, 25), gm, preferred_element_type=F32).astype(BF16)
    lt = lax.dot_general(rows_l, gm, (((1,), (1,)), ((), ())), preferred_element_type=F32) / CB
    cols_r = lax.dot_general(
        pick(CB, 160, 40, 20, 25, 20), gm, (((1,), (1,)), ((), ())), preferred_element_type=F32).astype(BF16)
    rt = jnp.dot(cols_r, gm, preferred_element_type=F32) / BR
    for e in (2, 1, 3):
        a = lt[48 * e:48 * e + 48]
        b = rt[48 * e:48 * e + 48]
        sp[e - 1, :, pl.ds(0, 640)] = (a[:, :640] + b).astype(BF16)
        tail = a[:, 768:800]
        none = jnp.zeros((25, 32), F32)
        first = jnp.concatenate([none, tail[:20], none[:3]], axis=0)
        second = jnp.concatenate([none, tail[20:25], none[:18]], axis=0)
        both = jnp.concatenate([first, second, jnp.zeros((48, 64), F32)], axis=1)
        sp[e - 1, :, pl.ds(640, 128)] = (a[:, 640:768] + both).astype(BF16)
    st = {}
    for e in (2, 1, 3):
        st[e] = send(sp.at[e - 1], rp.at[e - 1], at_zh(e))
    lt4[zh, pl.ds(0, 25), :] = lt[:25]
    rt4[zh, pl.ds(0, 20), :] = rt[25:45]
    sel = (lax.broadcasted_iota(jnp.int32, (80, CB), 1)
           == lax.broadcasted_iota(jnp.int32, (80, CB), 0) + (2 * x + k) * 80)
    gd_ref[...] = lax.dot_general(
        sel.astype(F32).astype(BF16), gm, (((1,), (1,)), ((), ())), preferred_element_type=F32).astype(BF16)

    w_core[1].wait_recv()
    dh_step(1, False)
    w_core[3].wait_recv()
    dh_step(3, False)
    w_to_core(2)
    w_core[2].wait_recv()
    stores = []
    for i in range(2):
        c = cot[2, pl.ds(i * 2, 2)].reshape(256, CB)
        rows = pl.ds(i * 256, 256)
        dh = (acc[rows, :] + jnp.dot(c, wt[2].reshape(CB, BR), preferred_element_type=F32)).T
        gu[:, rows] = (dh * act[:, rows]).astype(BF16)
        gg[:, rows] = (dh * fac[:, rows]).astype(BF16)
        for r in (2 * i, 2 * i + 1):
            col = pl.multiple_of(((zl + r) % 4) * 128, 128)
            a = pltpu.make_async_copy(gg.at[:, pl.ds(r * 128, 128)], gg_h.at[:, pl.ds(col, 128)], lsem.at[13 + r])
            b = pltpu.make_async_copy(gu.at[:, pl.ds(r * 128, 128)], gu_h.at[:, pl.ds(col, 128)], lsem.at[17 + r])
            a.start()
            b.start()
            stores += [a, b]

    for e in (1, 3, 2):
        st[e].wait_recv()
        c = (zh + 4 - e) % 4
        v = rp[e - 1].astype(F32)
        lt4[c, pl.ds(0, 25), pl.ds(0, 768)] = v[:25]
        lt4[c, pl.ds(0, 20), pl.ds(768, 32)] = v[25:45, 640:672]
        lt4[c, pl.ds(20, 5), pl.ds(768, 32)] = v[25:30, 672:704]
        rt4[c, pl.ds(0, 20), :] = v[25:45, :640]
    for c in range(4):
        left_ref[:, c, :] = lt4[c, pl.ds(0, 25), :]
        right_ref[:, c, :] = rt4[c, pl.ds(0, 20), :]

    for c in stores:
        c.wait()
    for c in sent:
        c.wait_send()
    for o in ORDER:
        for j in (1, 2, 3):
            for d in (1, -1):
                @pl.when(line_sends(o, j, d))
                def _(o=o, j=j, d=d):
                    line_copy(o, j, d).wait_send()
    assert count[0] <= NSEM


def place(*refs):
    n = len(refs) // 3
    held, sem = refs[2 * n:3 * n], refs[3 * n]
    into = [pltpu.make_async_copy(refs[i], held[i], sem.at[i]) for i in range(n)]
    out = [pltpu.make_async_copy(held[i], refs[n + i], sem.at[n + i]) for i in range(n)]
    for c in into:
        c.start()
    for c, d in zip(into, out):
        c.wait()
        d.start()
    for d in out:
        d.wait()


def body(gate_pre, up_pre, cotangent, down_weight):
    anyspec = pl.BlockSpec(memory_space=pl.ANY)
    vspec = pl.BlockSpec(memory_space=pltpu.VMEM)
    v = pltpu.VMEM
    out = pl.pallas_call(
        kernel,
        out_shape=(
            jax.ShapeDtypeStruct((BR, TOK), BF16),
            jax.ShapeDtypeStruct((BR, TOK), BF16),
            jax.ShapeDtypeStruct((80, BR), BF16),
            jax.ShapeDtypeStruct((25, 4, BR), F32),
            jax.ShapeDtypeStruct((20, 4, CB), F32),
        ),
        in_specs=[anyspec] * 4,
        out_specs=(anyspec, anyspec, vspec, vspec, vspec),
        scratch_shapes=[
            v((BR, TOK), BF16),
            v((BR, TOK), BF16),
            v((4, 4, 4, 32, CB), BF16),
            v((BR, TOK), BF16),
            v((BR, TOK), F32),
            v((BR, TOK), F32),
            v((4, 4, 2, 80, BR), BF16),
            v((4, 4096, 128), BF16),
            v((4, 2048, 128), BF16),
            v((4, 2048, 128), BF16),
            v((4, 3, 512, 128), BF16),
            v((3, 512, 128), BF16),
            v((2, 512, 128), BF16),
            v((2, 512, 128), BF16),
            v((4096, 128), BF16),
            v((BR, CB), BF16),
            v((3, 48, 768), BF16),
            v((3, 48, 768), BF16),
            v((4, 32, BR), F32),
            v((4, 32, CB), F32),
            v((TOK, BR), F32),
            v((BR, TOK), BF16),
            v((BR, TOK), BF16),
            pltpu.SemaphoreType.DMA((NSEM,)),
            pltpu.SemaphoreType.DMA((NSEM,)),
            pltpu.SemaphoreType.DMA((21,)),
        ],
        compiler_params=pltpu.CompilerParams(
            collective_id=0, has_side_effects=True, vmem_limit_bytes=56 * 2**20),
        cost_estimate=pl.CostEstimate(flops=4_600_000_000, bytes_accessed=6_000_000, transcendentals=410_000),
    )(gate_pre.T, up_pre.T, cotangent, down_weight.T)
    out = pl.pallas_call(
        place,
        out_shape=tuple(jax.ShapeDtypeStruct(o.shape, o.dtype) for o in out),
        in_specs=[anyspec] * 5,
        out_specs=(anyspec,) * 5,
        scratch_shapes=[v(o.shape, o.dtype) for o in out] + [pltpu.SemaphoreType.DMA((10,))],
        compiler_params=pltpu.CompilerParams(vmem_limit_bytes=56 * 2**20),
    )(*out)
    return (out[0].T, out[1].T, out[2].T,
            out[3].transpose(1, 0, 2)[None], out[4].transpose(1, 0, 2)[None])


def solution(mesh):
    return jax.shard_map(
        body,
        mesh=mesh,
        in_specs=(
            P("dp", "tensor"),
            P("dp", "tensor"),
            P(("dp", "tensor"), None),
            P("tensor", "dp"),
        ),
        out_specs=(
            P("dp", "tensor"),
            P("dp", "tensor"),
            P("tensor", "dp"),
            P("tensor", None, "dp", None),
            P("tensor", None, "dp", None),
        ),
        check_vma=False,
    )
```
